128 devices in a mesh: dev: 128 (over x, z, y, core).
Axes of the slice: x: 4, y: 4, z: 4, core: 2. Of those that a mesh axis runs over, the one named last changes fastest.
Arguments:
- embeddings: float32 [131072, 200], P('dev')
- node_state: float32 [131072], P('dev'), may hold values from 0.01 to 1
- relations: float32 [14336, 200], replicated, may hold values from 0.1 to 1.9
- relation_state: float32 [14336], replicated, may hold values from 0.01 to 1
- plan: int32 [1], replicated, may hold values from 1 to 127
- edge_count: int32 [128], P('dev'), may hold values from 1 to 2048, 163840 in all
- sources: int32 [262144], P('dev'), may hold values from 0 to 1023
- targets: int32 [262144], P('dev'), may hold values from 0 to 1023
- relation_ids: int32 [262144], P('dev'), may hold values from 0 to 14335
- negatives: int32 [256, 1024], P('dev'), may hold values from 0 to 1023
Outputs:
- new_embeddings: float32 [131072, 200], P('dev')
- new_node_state: float32 [131072], P('dev')
- new_relations: float32 [14336, 200], replicated
- new_relation_state: float32 [14336], replicated
The draws below stay inside these ranges and needn't reach their ends.
Inputs may be any that keep to these rules, and one draw needn't show every extreme that they name: `edge_count`: the busiest bucket is full: its count is 2048.
All inputs are finite; a program needn't handle non-finite values. No bound on the sum of `edge_count` on one device may be relied on, other than what follows from the above.
Results may differ from the reference program's by a relative error of at most 0.0003.
Values sent between devices are 32-bit elements; how exact they have to be, the bound alone decides.
A program may use at most 192 MiB of HBM per device.

```python
import math
import jax
import jax.numpy as jnp
import numpy as np
from jax import lax

D = 200
REL = 14336
NEG = 1024
NODES_DEV = 1024
EDGES_DEV = 2048
NODES_ALL = 131072
EDGES_ALL = 262144
SPANS = 2
SPANS_ALL = 256
N_DEV = 128


def draw_embeddings(key, part):
    key = jax.random.fold_in(key, 7)
    noise_key = jax.random.fold_in(key, 0)
    sample = jnp.clip(jax.random.normal(noise_key, (NODES_ALL, D), jnp.float32), -4.0, 4.0) * 0.3
    return sample


def with_ends(entries, own_key, least, largest):
    spot = [jax.random.randint(jax.random.fold_in(own_key, axis), (), 0, length) for axis, length in enumerate(entries.shape)]
    longest = entries.shape.index(max(entries.shape))
    neighbour = spot[:longest] + [(spot[longest] + 1) % entries.shape[longest]] + spot[longest + 1:]
    return entries.at[tuple(spot)].set(least).at[tuple(neighbour)].set(largest)


def shard_levels(key, shape, shards, low, largest):
    loudness, own = 1.0, jax.random.fold_in(key, 6)
    for axis_at, blocks in shards:
        draws = jnp.exp(jax.random.uniform(jax.random.fold_in(own, axis_at), (blocks,), jnp.float32, low / len(shards), largest / len(shards)))
        loudness = loudness * jnp.repeat(draws, shape[axis_at] // blocks).reshape([-1 if axis == axis_at else 1 for axis in range(len(shape))])
    return loudness


def cumulative_ranks(count, skew):
    weights = [(1 << 20) // math.isqrt(rank ** skew) + 1 for rank in range(1, count + 1)]
    deviation = 1 + sum(weights) // (1 << 30)
    return np.cumsum(np.array([max(1, weight // deviation) for weight in weights]))


def ranked(own_key, extent, count, skew):
    grid = cumulative_ranks(count, skew)
    ticket = jax.random.randint(jax.random.fold_in(own_key, 1), extent, 0, int(grid[count - 1]))
    standing = jnp.searchsorted(jnp.asarray(grid, jnp.int32), ticket, side="right")
    return jax.random.permutation(jax.random.fold_in(own_key, 2), count)[standing].astype(jnp.int32)


def profile(amount, total, most, slope):
    loads = [(1 << 20) // math.isqrt(rank ** slope) + 1 for rank in range(2, amount + 1)]
    spare, holding = total - most - (amount - 1), [1] * (amount - 1)
    while spare > 0:
        movable = [i for i in range(amount - 1) if holding[i] < most]
        whole, left = sum([loads[i] for i in movable]), spare
        for i in movable:
            extra = min(most - holding[i], max(1, left * loads[i] // whole), spare)
            holding[i] = holding[i] + extra
            spare = spare - extra
    return np.array([most] + holding)


def uneven_parts(rng, count, total, reach, skew):
    if count == 2:
        one = jax.random.randint(rng, (), max(1, total - reach), min(reach, total - 1) + 1)
        return jnp.stack([one, total - one])
    tallies = jnp.asarray(profile(count, total, reach, skew), jnp.int32)
    couples = (count - 1) // 2
    giver, receiver = tallies[1:1 + 2 * couples:2], tallies[2:2 + 2 * couples:2]
    room = jnp.minimum(giver - 1, reach - receiver)
    moved = jax.random.randint(jax.random.fold_in(rng, 1), (couples,), 0, 1 << 20) % (room + 1)
    tallies = tallies.at[1:1 + 2 * couples:2].set(giver - moved).at[2:2 + 2 * couples:2].set(receiver + moved)
    return tallies[jax.random.permutation(jax.random.fold_in(rng, 2), count)]


def setup_inputs(seed: int = 0) -> dict:
    splits = jax.random.split(jax.random.key(seed), 11)
    return {
        "embeddings": draw_embeddings(jax.random.fold_in(splits[10], 71), 0),
        "node_state": jnp.clip(jnp.exp(math.log(1.0) - 4.6051702 * jax.random.uniform(splits[1], (NODES_ALL,), jnp.float32) ** shard_levels(splits[1], (NODES_ALL,), ((0, 128),), -0.2, 0.2)), 0.01, 1.0),
        "relations": jnp.clip(1.0 + 0.18 * jax.random.normal(splits[2], (REL, D), jnp.float32), 0.1, 1.9),
        "relation_state": jnp.clip(jnp.exp(jax.random.uniform(splits[3], (REL,), jnp.float32, math.log(0.01), math.log(1.0))), 0.01, 1.0),
        "plan": jax.random.randint(splits[4], (1,), 1, N_DEV).astype(jnp.int32),
        "edge_count": uneven_parts(splits[5], N_DEV, N_DEV * EDGES_DEV * 5 // 8, EDGES_DEV, 2).astype(jnp.int32),
        "sources": with_ends(jax.random.randint(splits[6], (EDGES_ALL,), 0, NODES_DEV), jax.random.fold_in(splits[6], 1), 0, NODES_DEV - 1).astype(jnp.int32),
        "targets": with_ends(jax.random.randint(splits[7], (EDGES_ALL,), 0, NODES_DEV), jax.random.fold_in(splits[7], 1), 0, NODES_DEV - 1).astype(jnp.int32),
        "relation_ids": with_ends(ranked(splits[8], (EDGES_ALL,), REL, 2), jax.random.fold_in(splits[8], 3), 0, REL - 1).astype(jnp.int32),
        "negatives": with_ends(jax.random.randint(splits[9], (SPANS_ALL, NEG), 0, NODES_DEV), jax.random.fold_in(splits[9], 1), 0, NODES_DEV - 1).astype(jnp.int32),
    }


learn_rate = 0.1
epsilon = 1e-06

def bucket_loss(left_block, right_block, rel_table, sources, targets, relation_ids, negatives, live_edges):
    queries = left_block[sources] * rel_table[relation_ids]
    positive = lax.optimization_barrier(jnp.sum(queries * right_block[targets], axis=-1))
    blocks = negatives.shape[0]
    grouped = queries.reshape(blocks, -1, queries.shape[-1])
    neg_rows = right_block[negatives]
    negative = jnp.einsum('cnd,ckd->cnk', grouped, neg_rows, precision=lax.Precision.HIGHEST)
    positive = positive.reshape(blocks, -1)
    highest = jnp.maximum(positive, lax.optimization_barrier(jnp.max(negative, axis=-1)))
    log_total = highest + jnp.log(jnp.exp(positive - highest) + lax.optimization_barrier(jnp.sum(jnp.exp(negative - highest[..., None]), axis=-1)))
    slot_index = jnp.arange(sources.shape[0], dtype=jnp.int32).reshape(blocks, -1)
    is_live = slot_index < live_edges
    return jnp.sum(jnp.where(is_live, log_total - positive, 0.0))

def adagrad(weights, squares, gradient):
    new_squares = squares + lax.optimization_barrier(jnp.mean(gradient * gradient, axis=-1))
    return (weights - learn_rate * gradient / (jnp.sqrt(new_squares)[..., None] + epsilon), new_squares)

def reference(embeddings, node_state, relations, relation_state, plan, edge_count, sources, targets, relation_ids, negatives):
    blocks = embeddings.reshape(N_DEV, NODES_DEV, D)
    flip_mask = plan[0]

    def accumulate(running, device):
        node_grad, rel_grad = running
        partner = jnp.bitwise_xor(device, flip_mask)
        left_block = blocks[device]
        right_block = blocks[partner]
        edge_src = lax.dynamic_slice_in_dim(sources, device * EDGES_DEV, EDGES_DEV)
        edge_dst = lax.dynamic_slice_in_dim(targets, device * EDGES_DEV, EDGES_DEV)
        edge_rel = lax.dynamic_slice_in_dim(relation_ids, device * EDGES_DEV, EDGES_DEV)
        neg_ids = lax.dynamic_slice_in_dim(negatives, device * SPANS, SPANS, 0)
        left_grad, right_grad, table_grad = jax.grad(bucket_loss, argnums=(0, 1, 2))(left_block, right_block, relations, edge_src, edge_dst, edge_rel, neg_ids, edge_count[device])
        node_grad = node_grad.at[device].add(left_grad).at[partner].add(right_grad)
        return ((node_grad, rel_grad + table_grad), None)
    start_grads = (jnp.zeros(blocks.shape, embeddings.dtype), jnp.zeros(relations.shape, relations.dtype))
    (node_grad, rel_grad), _ = lax.scan(accumulate, start_grads, jnp.arange(N_DEV, dtype=jnp.int32))
    new_embeddings, new_node_state = adagrad(embeddings, node_state, node_grad.reshape(embeddings.shape))
    new_relations, new_relation_state = adagrad(relations, relation_state, rel_grad)
    return (new_embeddings, new_node_state, new_relations, new_relation_state)
```

```python
import jax
import jax.numpy as jnp
from jax import lax
from jax.sharding import PartitionSpec as P

learn_rate = 0.1
epsilon = 1e-06


def bucket_loss(
    left_block, right_block, rel_table, sources, targets, relation_ids, negatives, live_edges
):
    queries = left_block[sources] * rel_table[relation_ids]
    positive = jnp.sum(queries * right_block[targets], axis=-1)
    blocks = negatives.shape[0]
    grouped = queries.reshape(blocks, -1, queries.shape[-1])
    neg_rows = right_block[negatives]
    negative = jnp.einsum("cnd,ckd->cnk", grouped, neg_rows, precision=lax.Precision.HIGHEST)
    positive = positive.reshape(blocks, -1)
    highest = jnp.maximum(positive, jnp.max(negative, axis=-1))
    log_total = highest + jnp.log(
        jnp.exp(positive - highest) + jnp.sum(jnp.exp(negative - highest[..., None]), axis=-1)
    )
    slot_index = jnp.arange(sources.shape[0], dtype=jnp.int32).reshape(blocks, -1)
    is_live = slot_index < live_edges
    return jnp.sum(jnp.where(is_live, log_total - positive, 0.0))


def adagrad(weights, squares, gradient):
    new_squares = squares + jnp.mean(gradient * gradient, axis=-1)
    return (
        weights - learn_rate * gradient / (jnp.sqrt(new_squares)[..., None] + epsilon),
        new_squares,
    )


def partner_block(payload, flip_mask):
    def by(mask):
        pairs = [(i, i ^ mask) for i in range(lax.axis_size("dev"))]
        return lambda block: lax.ppermute(block, "dev", pairs)

    branches = [by(mask) for mask in range(1, lax.axis_size("dev"))]
    return lax.switch(flip_mask - 1, branches, payload)


def shards(
    embeddings,
    node_state,
    relations,
    relation_state,
    plan,
    edge_count,
    sources,
    targets,
    relation_ids,
    negatives,
):
    flip_mask = plan[0]
    fetched = partner_block(embeddings, flip_mask)
    left_grad, right_grad, table_grad = jax.grad(bucket_loss, argnums=(0, 1, 2))(
        embeddings, fetched, relations, sources, targets, relation_ids, negatives, edge_count[0]
    )
    returned = partner_block(right_grad, flip_mask)
    new_embeddings, new_node_state = adagrad(embeddings, node_state, left_grad + returned)
    summed = lax.psum(table_grad, "dev")
    new_relations, new_relation_state = adagrad(relations, relation_state, summed)
    return (new_embeddings, new_node_state, new_relations, new_relation_state)


def solution(mesh):
    return jax.shard_map(
        shards,
        mesh=mesh,
        in_specs=(
            P("dev", None),
            P("dev"),
            P(),
            P(),
            P(),
            P("dev"),
            P("dev"),
            P("dev"),
            P("dev"),
            P("dev", None),
        ),
        out_specs=(P("dev", None), P("dev"), P(), P()),
        check_vma=False,
    )
```

```python
import functools

import jax
import jax.numpy as jnp
from jax import lax
from jax.experimental import pallas as pl
from jax.experimental.pallas import tpu as pltpu
from jax.sharding import PartitionSpec as P

learn_rate = 0.1
epsilon = 1e-06

F32 = jnp.float32
BF16 = jnp.bfloat16
MESH = pl.DeviceIdType.MESH
D = 200
WIDE = 256
REL = 14336
NODES = 1024
EDGES = 2048
LANES = 128
TAIL = D - LANES
CHUNK = 256
TABLE_STEP = 1024

PARTS = ((5, ("x", "z", "y")), (5, ("z", "y", "x")), (4, ("y", "x", "z")))
STRIDE = {"x": 32, "z": 8, "y": 2}
TILES = tuple(n + 3 for n, _ in PARTS)
BASE = (0, 40, 80)
ROWS = 208


def split2(x):
    high = x.astype(BF16)
    return high, (x - high.astype(F32)).astype(BF16)


def dot(a, b):
    return jnp.dot(a, b, preferred_element_type=F32)


def dot_nt(a, b):
    return lax.dot_general(a, b, (((1,), (1,)), ((), ())), preferred_element_type=F32)


def gather_kernel(ids, table_t, rows, buf, table, sems):
    steps = REL // TABLE_STEP
    copies = []
    for j in range(steps):
        copy = pltpu.make_async_copy(
            table_t.at[:, pl.ds(j * TABLE_STEP, TABLE_STEP)], buf.at[j], sems.at[j]
        )
        copy.start()
        copies.append(copy)
    for j in range(steps):
        copies[j].wait()

        def turn(b, carry):
            lanes = pl.ds(pl.multiple_of(b * LANES, LANES), LANES)
            at = pl.ds(pl.multiple_of(j * TABLE_STEP + b * LANES, LANES), LANES)
            table[at, 0:LANES] = buf[j, 0:LANES, lanes].T
            low = jnp.concatenate(
                [buf[j, LANES:D, lanes], jnp.zeros((WIDE - D, LANES), F32)], axis=0
            )
            table[at, LANES:WIDE] = low.T
            return carry

        lax.fori_loop(0, TABLE_STEP // LANES, turn, 0)

    def fetch(step, carry):
        first = pl.multiple_of(step * 16, 16)
        for k in range(16):
            rows[pl.ds(first + k, 1), :] = table[pl.ds(ids[first + k], 1), :]
        return carry

    lax.fori_loop(0, EDGES // 16, fetch, 0)


def gather_rows(relation_ids, table_t):
    return pl.pallas_call(
        gather_kernel,
        out_shape=jax.ShapeDtypeStruct((EDGES, WIDE), F32),
        in_specs=[
            pl.BlockSpec(memory_space=pltpu.SMEM),
            pl.BlockSpec(memory_space=pl.ANY),
        ],
        out_specs=pl.BlockSpec(memory_space=pltpu.VMEM),
        scratch_shapes=[
            pltpu.VMEM((REL // TABLE_STEP, D, TABLE_STEP), F32),
            pltpu.VMEM((REL, WIDE), F32),
            pltpu.SemaphoreType.DMA((REL // TABLE_STEP,)),
        ],
        compiler_params=pltpu.CompilerParams(vmem_limit_bytes=48 << 20),
        name="gather_rows",
    )(relation_ids, table_t)


def column(row):
    return jnp.broadcast_to(row, (LANES, LANES)).T


def one_hot_pieces(row, width):
    ids = column(row)
    lane = lax.broadcasted_iota(jnp.int32, (LANES, LANES), 1)
    return [ids == lane + j * LANES for j in range(width // LANES)]


def one_hot(rows):
    return jnp.concatenate(
        [jnp.concatenate(one_hot_pieces(row, NODES), axis=1) for row in rows], axis=0
    )


def gradient_kernel(
    ids, live, left_t, right_t, rel_rows, sources, targets, negatives,
    left_grad, right_grad, g0, g1, g2,
    left_hi, left_lo, right_hi, right_lo, counts, rel_grad, table,
):
    def clear(step, carry):
        table[pl.ds(pl.multiple_of(step * 512, 512), 512), :] = jnp.zeros((512, WIDE), F32)
        return carry

    lax.fori_loop(0, REL // 512, clear, 0)

    pad = jnp.zeros((WIDE - D, NODES), BF16)
    for source, hi, lo in ((left_t, left_hi, left_lo), (right_t, right_hi, right_lo)):
        high, low = split2(source[...])
        hi[0:D, :] = high
        lo[0:D, :] = low
        hi[D:WIDE, :] = pad
        lo[D:WIDE, :] = pad
    left_grad[...] = jnp.zeros_like(left_grad)
    right_grad[...] = jnp.zeros_like(right_grad)

    for span in range(2):
        counts[span : span + 1, :] = jnp.zeros((1, NODES), F32)

        def count(k, carry):
            pieces = one_hot_pieces(negatives[pl.ds(span * 8 + k, 1), :], NODES)
            counts[span : span + 1, :] += jnp.concatenate(
                [jnp.sum(p.astype(F32), axis=0, keepdims=True) for p in pieces], axis=1
            )
            return carry

        lax.fori_loop(0, 8, count, 0)

    def chunk(step, carry):
        first = pl.multiple_of(step * CHUNK, CHUNK)
        edges = pl.ds(first, CHUNK)
        source_hot = one_hot([sources[pl.ds(step * 2 + h, 1), :] for h in range(2)])
        target_hot = one_hot([targets[pl.ds(step * 2 + h, 1), :] for h in range(2)])
        from_source = source_hot.astype(F32).astype(BF16)
        from_target = target_hot.astype(F32)

        rel = rel_rows[edges, :]
        left = dot_nt(from_source, left_hi[...]) + dot_nt(from_source, left_lo[...])
        query = left * rel
        q_hi, q_lo = split2(query)
        score = (
            dot(q_hi, right_hi[...]) + dot(q_hi, right_lo[...]) + dot(q_lo, right_hi[...])
        )

        span = step // (NODES // CHUNK)
        weight = counts[pl.ds(span, 1), :] + from_target
        score = jnp.where(weight > 0, score, -3e38)
        top = jnp.max(score, axis=1, keepdims=True)
        grown = weight * jnp.exp(score - top)
        total = jnp.sum(grown, axis=1, keepdims=True)
        slot = first + lax.broadcasted_iota(jnp.int32, (CHUNK, 1), 0)
        alive = (slot < live[0]).astype(F32)
        grad = grown * (alive / total) - from_target * alive

        d_hi, d_lo = split2(grad)
        d_query = (
            dot_nt(d_hi, right_hi[...]) + dot_nt(d_lo, right_hi[...]) + dot_nt(d_hi, right_lo[...])
        )
        rel_grad[edges, :] = d_query * left
        d_left = d_query * rel
        query_t = query.T[0:D, :]
        qt_hi, qt_lo = split2(query_t)
        right_grad[...] += dot(qt_hi, d_hi) + dot(qt_lo, d_hi) + dot(qt_hi, d_lo)
        lt_hi, lt_lo = split2(d_left.T[0:D, :])
        left_grad[...] += dot(lt_hi, from_source) + dot(lt_lo, from_source)
        return carry

    lax.fori_loop(0, EDGES // CHUNK, chunk, 0)

    def scatter(step, carry):
        first = pl.multiple_of(step * 16, 16)
        for k in range(16):
            at = pl.ds(ids[first + k], 1)
            table[at, :] += rel_grad[pl.ds(first + k, 1), :]
        return carry

    lax.fori_loop(0, EDGES // 16, scatter, 0)

    lane = lax.broadcasted_iota(jnp.int32, (LANES, LANES), 1)
    for part, out in enumerate((g0, g1, g2)):
        blocks = PARTS[part][0]

        def pack(group, carry):
            tails = []
            for block in range(blocks):
                at = pl.ds(
                    pl.multiple_of((BASE[part] + group * blocks + block) * LANES, LANES), LANES
                )
                out[group, :, block * 8 : block * 8 + 8, :] = table[at, 0:LANES].reshape(16, 8, LANES)
                tail = table[at, LANES:WIDE]
                tails.append(pltpu.roll(tail, (TAIL * block) % LANES, 1) if block else tail)
            packed = [
                tails[0] + jnp.where(lane >= 72, tails[1], 0.0),
                jnp.where(lane < 16, tails[1], 0.0) + tails[2] + jnp.where(lane >= 88, tails[3], 0.0),
                jnp.where(lane < 32, tails[3], 0.0),
            ]
            if blocks == 5:
                packed[2] = packed[2] + tails[4]
            for j in range(3):
                at = (blocks + j) * 8
                out[group, :, at : at + 8, :] = packed[j].reshape(16, 8, LANES)
            return carry

        lax.fori_loop(0, 8, pack, 0)


def bucket_gradients(relation_ids, live, left_t, right_t, rel_rows, sources, targets, negatives):
    vmem = pl.BlockSpec(memory_space=pltpu.VMEM)
    smem = pl.BlockSpec(memory_space=pltpu.SMEM)
    packed = [jax.ShapeDtypeStruct((8, 16, tiles * 8, LANES), F32) for tiles in TILES]
    return pl.pallas_call(
        gradient_kernel,
        out_shape=[
            jax.ShapeDtypeStruct((D, NODES), F32),
            jax.ShapeDtypeStruct((D, NODES), F32),
            *packed,
        ],
        in_specs=[smem, smem] + [vmem] * 6,
        out_specs=[vmem] * 5,
        scratch_shapes=[
            pltpu.VMEM((WIDE, NODES), BF16),
            pltpu.VMEM((WIDE, NODES), BF16),
            pltpu.VMEM((WIDE, NODES), BF16),
            pltpu.VMEM((WIDE, NODES), BF16),
            pltpu.VMEM((2, NODES), F32),
            pltpu.VMEM((EDGES, WIDE), F32),
            pltpu.VMEM((REL, WIDE), F32),
        ],
        compiler_params=pltpu.CompilerParams(vmem_limit_bytes=56 << 20),
        name="bucket_gradients",
    )(
        relation_ids, live, left_t, right_t, rel_rows,
        sources.reshape(16, LANES), targets.reshape(16, LANES), negatives.reshape(16, LANES),
    )


def table_kernel(
    g0, g1, g2, weights_t, states, out,
    own0, own1, own2, pair0, pair1, pair2, r10, r11, r12, r20, r21, r22, r30, r31, r32,
    f0, f1, f2, c0, c1, c2, w0, w1, w2, local_sems, send_sems, recv_sems,
):
    me = lax.axis_index("dev")
    core = lax.rem(me, 2)
    where = {"y": lax.rem(me // 2, 4), "z": lax.rem(me // 8, 4), "x": me // 32}
    sibling = me + 1 - 2 * core
    grads, own, pair = (g0, g1, g2), (own0, own1, own2), (pair0, pair1, pair2)
    first, second, third = (r10, r11, r12), (r20, r21, r22), (r30, r31, r32)
    full, ready, weight = (f0, f1, f2), (c0, c1, c2), (w0, w1, w2)

    def ahead(axis, k):
        return lax.rem(where[axis] + k, 4)

    def peer(axis, k):
        return me + (ahead(axis, k) - where[axis]) * STRIDE[axis]

    used = [0]

    def remote(src, dst, to):
        i = used[0]
        used[0] += 1
        copy = pltpu.make_async_remote_copy(
            src_ref=src, dst_ref=dst, send_sem=send_sems.at[i], recv_sem=recv_sems.at[i],
            device_id=(to,), device_id_type=MESH,
        )
        copy.start()
        return copy

    def add(target, row0, rows, terms):
        step = rows // 8 if rows % 64 == 0 else rows

        def body(s, carry):
            at = pl.ds(pl.multiple_of(s * step, 8), step)
            total = terms[0](at)
            for term in terms[1:]:
                total = total + term(at)
            target(at, total)
            return carry

        lax.fori_loop(0, rows // step, body, 0)

    def group_lanes(part, at_first, at_core):
        blocks = PARTS[part][0]
        block = BASE[part] + (at_core * 4 + at_first) * blocks
        return pl.ds(pl.multiple_of(block * LANES, LANES), blocks * LANES)

    local = []
    for p in range(3):
        copy = pltpu.make_async_copy(grads[p].at[core], own[p], local_sems.at[p])
        copy.start()
        local.append(copy)
    fetch = []
    for p, (blocks, axes) in enumerate(PARTS):
        copy = pltpu.make_async_copy(
            weights_t.at[:, group_lanes(p, where[axes[0]], core)], weight[p], local_sems.at[3 + p]
        )
        copy.start()
        fetch.append(copy)

    barrier = pltpu.get_barrier_semaphore()
    pl.semaphore_signal(barrier, inc=1, device_id=(sibling,), device_id_type=MESH)
    for axis in ("x", "z", "y"):
        for k in (1, 2, 3):
            pl.semaphore_signal(barrier, inc=1, device_id=(peer(axis, k),), device_id_type=MESH)
    pl.semaphore_wait(barrier, 10)

    halves = {}
    for k in (2, 1, 3, 0):
        for p, (blocks, axes) in enumerate(PARTS):
            at = ahead(axes[0], k)
            halves[k, p] = remote(grads[p].at[1 - core, at], pair[p].at[at], sibling)
    for copy in local:
        copy.wait()

    sent = []
    firsts = {}
    for k in (2, 1, 3, 0):
        for p, (blocks, axes) in enumerate(PARTS):
            at = ahead(axes[0], k)
            halves[k, p].wait_recv()
            rows = 16 * TILES[p] * 8
            mine, theirs = own[p], pair[p]

            def store(s, value, mine=mine, at=at):
                mine[at, s, :] = value

            add(store, 0, rows, [
                lambda s, mine=mine, at=at: mine[at, s, :],
                lambda s, theirs=theirs, at=at: theirs[at, s, :],
            ])
            if k:
                firsts[k, p] = remote(own[p].at[at], first[p].at[k - 1], peer(axes[0], k))

    seconds = {}
    for p, (blocks, axes) in enumerate(PARTS):
        at = where[axes[0]]
        for k in (1, 2, 3):
            firsts[k, p].wait_recv()
        rows = 16 * TILES[p] * 8
        mine, got = own[p], first[p]

        def store(s, value, mine=mine, at=at):
            mine[at, s, :] = value

        add(store, 0, rows, [lambda s, mine=mine, at=at: mine[at, s, :]] + [
            (lambda s, got=got, k=k: got[k, s, :]) for k in range(3)
        ])
        size = 4 * TILES[p] * 8
        for k in (2, 1, 3):
            rows_at = pl.ds(pl.multiple_of(ahead(axes[1], k) * size, 8), size)
            seconds[k, p] = remote(own[p].at[at, rows_at], second[p].at[k - 1], peer(axes[1], k))

    thirds = {}
    for p, (blocks, axes) in enumerate(PARTS):
        at = where[axes[0]]
        for k in (1, 2, 3):
            seconds[k, p].wait_recv()
        size = 4 * TILES[p] * 8
        base = where[axes[1]] * size
        mine, got = own[p], second[p]
        total = mine[at, pl.ds(pl.multiple_of(base, 8), size), :]
        for k in range(3):
            total = total + got[k]
        mine[at, pl.ds(pl.multiple_of(base, 8), size), :] = total
        small = TILES[p] * 8
        for k in (2, 1, 3):
            rows_at = pl.ds(pl.multiple_of(base + ahead(axes[2], k) * small, 8), small)
            thirds[k, p] = remote(own[p].at[at, rows_at], third[p].at[k - 1], peer(axes[2], k))

    backs = {}
    for p, (blocks, axes) in enumerate(PARTS):
        at = where[axes[0]]
        for k in (1, 2, 3):
            thirds[k, p].wait_recv()
        small = TILES[p] * 8
        row = where[axes[1]] * 4 + where[axes[2]]
        total = own[p][at, pl.ds(pl.multiple_of(row * small, 8), small), :]
        for k in range(3):
            total = total + third[p][k]
        full[p][row] = total
        for k in (2, 1, 3):
            backs[k, p] = remote(full[p].at[row], full[p].at[row], peer(axes[2], k))

    returns = {}
    for p, (blocks, axes) in enumerate(PARTS):
        for k in (1, 2, 3):
            backs[k, p].wait_recv()
        rows_at = pl.ds(where[axes[1]] * 4, 4)
        for k in (2, 1, 3):
            returns[k, p] = remote(full[p].at[rows_at], full[p].at[rows_at], peer(axes[1], k))

    lane = lax.broadcasted_iota(jnp.int32, (LANES, LANES), 1)
    lasts, across = {}, []
    stores = []
    for p, (blocks, axes) in enumerate(PARTS):
        for k in (1, 2, 3):
            returns[k, p].wait_recv()
        fetch[p].wait()
        tails = [full[p][:, (blocks + j) * 8 : (blocks + j) * 8 + 8, :].reshape(LANES, LANES) for j in range(3)]
        for block in range(blocks):
            head = full[p][:, block * 8 : block * 8 + 8, :].reshape(LANES, LANES)
            start = (TAIL * block) % LANES
            tile = (TAIL * block) // LANES
            tail = tails[tile]
            if start + TAIL > LANES:
                tail = jnp.where(lane >= start, tail, tails[tile + 1])
            if start:
                tail = pltpu.roll(tail, LANES - start, 1)
            grad = jnp.concatenate([head.T, tail.T[0:TAIL, :]], axis=0)
            lanes = slice(block * LANES, (block + 1) * LANES)
            at_block = BASE[p] + (core * 4 + where[axes[0]]) * blocks + block
            state = states[at_block] + jnp.sum(grad * grad, axis=0, keepdims=True) * (1.0 / D)
            new = weight[p][:, lanes] - learn_rate * grad / (jnp.sqrt(state) + epsilon)
            ready[p][0:D, lanes] = new
            ready[p][D:ROWS, lanes] = jnp.broadcast_to(state, (ROWS - D, LANES))
        place = group_lanes(p, where[axes[0]], core)
        for k in (2, 1, 3):
            lasts[k, p] = remote(ready[p], out.at[:, place], peer(axes[0], k))
        across.append(remote(ready[p], out.at[:, place], sibling))
        copy = pltpu.make_async_copy(ready[p], out.at[:, place], local_sems.at[6 + p])
        copy.start()
        stores.append(copy)

    for k in (1, 3, 2):
        for p, (blocks, axes) in enumerate(PARTS):
            lasts[k, p].wait_recv()
            place = group_lanes(p, ahead(axes[0], 4 - k), core)
            across.append(remote(out.at[:, place], out.at[:, place], sibling))
    for copy in across:
        copy.wait_recv()
    for copy in stores:
        copy.wait()
    for group in (halves, firsts, seconds, thirds, backs, returns, lasts):
        for copy in group.values():
            copy.wait_send()
    for copy in across:
        copy.wait_send()


def update_table(grads, weights_t, states):
    any_space = pl.BlockSpec(memory_space=pl.ANY)
    vmem = pl.BlockSpec(memory_space=pltpu.VMEM)
    rows = [16 * tiles * 8 for tiles in TILES]
    scratch = [pltpu.VMEM((4, r, LANES), F32) for r in rows] * 2
    scratch += [pltpu.VMEM((3, r, LANES), F32) for r in rows]
    scratch += [pltpu.VMEM((3, r // 4, LANES), F32) for r in rows]
    scratch += [pltpu.VMEM((3, r // 16, LANES), F32) for r in rows]
    scratch += [pltpu.VMEM((16, tiles * 8, LANES), F32) for tiles in TILES]
    scratch += [pltpu.VMEM((ROWS, n * LANES), F32) for n, _ in PARTS]
    scratch += [pltpu.VMEM((D, n * LANES), F32) for n, _ in PARTS]
    scratch += [
        pltpu.SemaphoreType.DMA((9,)),
        pltpu.SemaphoreType.DMA((78,)),
        pltpu.SemaphoreType.DMA((78,)),
    ]
    return pl.pallas_call(
        table_kernel,
        out_shape=jax.ShapeDtypeStruct((ROWS, REL), F32),
        in_specs=[any_space] * 4 + [vmem],
        out_specs=any_space,
        scratch_shapes=scratch,
        compiler_params=pltpu.CompilerParams(
            collective_id=0, has_side_effects=True, vmem_limit_bytes=40 << 20
        ),
        name="update_table",
    )(*grads, weights_t, states)


def exchange(payload, flip_mask):
    size = lax.axis_size("dev")

    def node(mask, bits):
        if bits == 0:
            if mask == 0:
                return lambda block: block
            pairs = [(i, i ^ mask) for i in range(size)]
            return lambda block: lax.ppermute(block, "dev", pairs)
        bit = bits - 1
        high, low = node(mask | 1 << bit, bit), node(mask, bit)
        return lambda block: lax.cond(
            jnp.bitwise_and(jnp.right_shift(flip_mask, bit), 1) == 1, high, low, block
        )

    return node(0, size.bit_length() - 1)(payload)


def shards(
    embeddings,
    node_state,
    relations,
    relation_state,
    plan,
    edge_count,
    sources,
    targets,
    relation_ids,
    negatives,
):
    flip_mask = plan[0]
    left_t = embeddings.T
    table_t = relations.T
    rel_rows = gather_rows(relation_ids, table_t)
    right_t = exchange(left_t, flip_mask)
    left_grad, right_grad, *packed = bucket_gradients(
        relation_ids, edge_count, left_t, right_t, rel_rows, sources, targets, negatives
    )
    grads = [
        g.reshape(2, 4, 16 * tiles * 8, LANES) for g, tiles in zip(packed, TILES)
    ]
    returned = exchange(right_grad, flip_mask)
    table = update_table(grads, table_t, relation_state.reshape(REL // LANES, 1, LANES))

    node_grad = left_grad + returned
    new_node_state = node_state + jnp.mean(node_grad * node_grad, axis=0)
    new_left = left_t - learn_rate * node_grad / (jnp.sqrt(new_node_state)[None, :] + epsilon)
    return (new_left.T, new_node_state, table[0:D].T, table[D])


def solution(mesh):
    return jax.shard_map(
        shards,
        mesh=mesh,
        in_specs=(
            P("dev", None),
            P("dev"),
            P(),
            P(),
            P(),
            P("dev"),
            P("dev"),
            P("dev"),
            P("dev"),
            P("dev", None),
        ),
        out_specs=(P("dev", None), P("dev"), P(), P()),
        check_vma=False,
    )
```

```python
import functools

import jax
import jax.numpy as jnp
from jax import lax
from jax.experimental import pallas as pl
from jax.experimental.pallas import tpu as pltpu
from jax.sharding import PartitionSpec as P

learn_rate = 0.1
epsilon = 1e-06

F32 = jnp.float32
BF16 = jnp.bfloat16
MESH = pl.DeviceIdType.MESH
D = 200
WIDE = 256
REL = 14336
NODES = 1024
EDGES = 2048
LANES = 128
TAIL = D - LANES
CHUNK = 256
TABLE_STEP = 1024

PARTS = ((5, ("x", "z", "y")), (5, ("z", "y", "x")), (4, ("y", "x", "z")))
STRIDE = {"x": 32, "z": 8, "y": 2}
TILES = tuple(n + 3 for n, _ in PARTS)
BASE = (0, 40, 80)
ROWS = 208


def split2(x):
    high = x.astype(BF16)
    return high, (x - high.astype(F32)).astype(BF16)


def dot(a, b):
    return jnp.dot(a, b, preferred_element_type=F32)


def dot_nt(a, b):
    return lax.dot_general(a, b, (((1,), (1,)), ((), ())), preferred_element_type=F32)


def gather_kernel(ids, table_t, rows, buf, table, sems):
    steps = REL // TABLE_STEP
    copies = []
    for j in range(steps):
        copy = pltpu.make_async_copy(
            table_t.at[:, pl.ds(j * TABLE_STEP, TABLE_STEP)], buf.at[j], sems.at[j]
        )
        copy.start()
        copies.append(copy)
    for j in range(steps):
        copies[j].wait()

        def turn(b, carry):
            lanes = pl.ds(pl.multiple_of(b * LANES, LANES), LANES)
            at = pl.ds(pl.multiple_of(j * TABLE_STEP + b * LANES, LANES), LANES)
            table[at, 0:LANES] = buf[j, 0:LANES, lanes].T
            low = jnp.concatenate(
                [buf[j, LANES:D, lanes], jnp.zeros((WIDE - D, LANES), F32)], axis=0
            )
            table[at, LANES:WIDE] = low.T
            return carry

        lax.fori_loop(0, TABLE_STEP // LANES, turn, 0)

    def fetch(step, carry):
        first = pl.multiple_of(step * 16, 16)
        for k in range(16):
            rows[pl.ds(first + k, 1), :] = table[pl.ds(ids[first + k], 1), :]
        return carry

    lax.fori_loop(0, EDGES // 16, fetch, 0)


def gather_rows(relation_ids, table_t):
    return pl.pallas_call(
        gather_kernel,
        out_shape=jax.ShapeDtypeStruct((EDGES, WIDE), F32),
        in_specs=[
            pl.BlockSpec(memory_space=pltpu.SMEM),
            pl.BlockSpec(memory_space=pl.ANY),
        ],
        out_specs=pl.BlockSpec(memory_space=pltpu.VMEM),
        scratch_shapes=[
            pltpu.VMEM((REL // TABLE_STEP, D, TABLE_STEP), F32),
            pltpu.VMEM((REL, WIDE), F32),
            pltpu.SemaphoreType.DMA((REL // TABLE_STEP,)),
        ],
        compiler_params=pltpu.CompilerParams(vmem_limit_bytes=48 << 20),
        name="gather_rows",
    )(relation_ids, table_t)


def column(row):
    return jnp.broadcast_to(row, (LANES, LANES)).T


def one_hot_pieces(row, width):
    ids = column(row)
    lane = lax.broadcasted_iota(jnp.int32, (LANES, LANES), 1)
    return [ids == lane + j * LANES for j in range(width // LANES)]


def one_hot(rows):
    return jnp.concatenate(
        [jnp.concatenate(one_hot_pieces(row, NODES), axis=1) for row in rows], axis=0
    )


def gradient_kernel(
    ids, live, left_t, right_t, rel_rows, sources, targets, negatives,
    left_grad, right_grad, g0, g1, g2,
    left_hi, left_lo, right_hi, right_lo, counts, rel_grad, table,
):
    def clear(step, carry):
        table[pl.ds(pl.multiple_of(step * 512, 512), 512), :] = jnp.zeros((512, WIDE), F32)
        return carry

    lax.fori_loop(0, REL // 512, clear, 0)

    pad = jnp.zeros((WIDE - D, NODES), BF16)
    for source, hi, lo in ((left_t, left_hi, left_lo), (right_t, right_hi, right_lo)):
        high, low = split2(source[...])
        hi[0:D, :] = high
        lo[0:D, :] = low
        hi[D:WIDE, :] = pad
        lo[D:WIDE, :] = pad
    left_grad[...] = jnp.zeros_like(left_grad)
    right_grad[...] = jnp.zeros_like(right_grad)

    for span in range(2):
        counts[span : span + 1, :] = jnp.zeros((1, NODES), F32)

        def count(k, carry):
            pieces = one_hot_pieces(negatives[pl.ds(span * 8 + k, 1), :], NODES)
            counts[span : span + 1, :] += jnp.concatenate(
                [jnp.sum(p.astype(F32), axis=0, keepdims=True) for p in pieces], axis=1
            )
            return carry

        lax.fori_loop(0, 8, count, 0)

    def chunk(step, carry):
        first = pl.multiple_of(step * CHUNK, CHUNK)
        edges = pl.ds(first, CHUNK)
        source_hot = one_hot([sources[pl.ds(step * 2 + h, 1), :] for h in range(2)])
        target_hot = one_hot([targets[pl.ds(step * 2 + h, 1), :] for h in range(2)])
        from_source = source_hot.astype(F32).astype(BF16)
        from_target = target_hot.astype(F32)

        rel = rel_rows[edges, :]
        left = dot_nt(from_source, left_hi[...]) + dot_nt(from_source, left_lo[...])
        query = left * rel
        q_hi, q_lo = split2(query)
        score = (
            dot(q_hi, right_hi[...]) + dot(q_hi, right_lo[...]) + dot(q_lo, right_hi[...])
        )

        span = step // (NODES // CHUNK)
        weight = counts[pl.ds(span, 1), :] + from_target
        score = jnp.where(weight > 0, score, -3e38)
        top = jnp.max(score, axis=1, keepdims=True)
        grown = weight * jnp.exp(score - top)
        total = jnp.sum(grown, axis=1, keepdims=True)
        slot = first + lax.broadcasted_iota(jnp.int32, (CHUNK, 1), 0)
        alive = (slot < live[0]).astype(F32)
        grad = grown * (alive / total) - from_target * alive

        d_hi, d_lo = split2(grad)
        d_query = (
            dot_nt(d_hi, right_hi[...]) + dot_nt(d_lo, right_hi[...]) + dot_nt(d_hi, right_lo[...])
        )
        rel_grad[edges, :] = d_query * left
        d_left = d_query * rel
        query_t = query.T[0:D, :]
        qt_hi, qt_lo = split2(query_t)
        right_grad[...] += dot(qt_hi, d_hi) + dot(qt_lo, d_hi) + dot(qt_hi, d_lo)
        lt_hi, lt_lo = split2(d_left.T[0:D, :])
        left_grad[...] += dot(lt_hi, from_source) + dot(lt_lo, from_source)
        return carry

    lax.fori_loop(0, EDGES // CHUNK, chunk, 0)

    def scatter(step, carry):
        first = pl.multiple_of(step * 16, 16)
        for k in range(16):
            at = pl.ds(ids[first + k], 1)
            table[at, :] += rel_grad[pl.ds(first + k, 1), :]
        return carry

    lax.fori_loop(0, EDGES // 16, scatter, 0)

    lane = lax.broadcasted_iota(jnp.int32, (LANES, LANES), 1)
    for part, out in enumerate((g0, g1, g2)):
        blocks = PARTS[part][0]

        def pack(group, carry):
            tails = []
            for block in range(blocks):
                at = pl.ds(
                    pl.multiple_of((BASE[part] + group * blocks + block) * LANES, LANES), LANES
                )
                out[group, :, block * 8 : block * 8 + 8, :] = table[at, 0:LANES].reshape(16, 8, LANES)
                tail = table[at, LANES:WIDE]
                tails.append(pltpu.roll(tail, (TAIL * block) % LANES, 1) if block else tail)
            packed = [
                tails[0] + jnp.where(lane >= 72, tails[1], 0.0),
                jnp.where(lane < 16, tails[1], 0.0) + tails[2] + jnp.where(lane >= 88, tails[3], 0.0),
                jnp.where(lane < 32, tails[3], 0.0),
            ]
            if blocks == 5:
                packed[2] = packed[2] + tails[4]
            for j in range(3):
                at = (blocks + j) * 8
                out[group, :, at : at + 8, :] = packed[j].reshape(16, 8, LANES)
            return carry

        lax.fori_loop(0, 8, pack, 0)


def bucket_gradients(relation_ids, live, left_t, right_t, rel_rows, sources, targets, negatives):
    vmem = pl.BlockSpec(memory_space=pltpu.VMEM)
    smem = pl.BlockSpec(memory_space=pltpu.SMEM)
    packed = [jax.ShapeDtypeStruct((8, 16, tiles * 8, LANES), F32) for tiles in TILES]
    return pl.pallas_call(
        gradient_kernel,
        out_shape=[
            jax.ShapeDtypeStruct((D, NODES), F32),
            jax.ShapeDtypeStruct((D, NODES), F32),
            *packed,
        ],
        in_specs=[smem, smem] + [vmem] * 6,
        out_specs=[vmem] * 5,
        scratch_shapes=[
            pltpu.VMEM((WIDE, NODES), BF16),
            pltpu.VMEM((WIDE, NODES), BF16),
            pltpu.VMEM((WIDE, NODES), BF16),
            pltpu.VMEM((WIDE, NODES), BF16),
            pltpu.VMEM((2, NODES), F32),
            pltpu.VMEM((EDGES, WIDE), F32),
            pltpu.VMEM((REL, WIDE), F32),
        ],
        compiler_params=pltpu.CompilerParams(vmem_limit_bytes=56 << 20),
        name="bucket_gradients",
    )(
        relation_ids, live, left_t, right_t, rel_rows,
        sources.reshape(16, LANES), targets.reshape(16, LANES), negatives.reshape(16, LANES),
    )


def table_kernel(
    g0, g1, g2, weights_t, states, out,
    own0, own1, own2, pair0, pair1, pair2, r10, r11, r12, r20, r21, r22, r30, r31, r32,
    f0, f1, f2, c0, c1, c2, w0, w1, w2, local_sems, send_sems, recv_sems,
):
    me = lax.axis_index("dev")
    core = lax.rem(me, 2)
    where = {"y": lax.rem(me // 2, 4), "z": lax.rem(me // 8, 4), "x": me // 32}
    sibling = me + 1 - 2 * core
    grads, own, pair = (g0, g1, g2), (own0, own1, own2), (pair0, pair1, pair2)
    first, second, third = (r10, r11, r12), (r20, r21, r22), (r30, r31, r32)
    full, ready, weight = (f0, f1, f2), (c0, c1, c2), (w0, w1, w2)

    def ahead(axis, k):
        return lax.rem(where[axis] + k, 4)

    def peer(axis, k):
        return me + (ahead(axis, k) - where[axis]) * STRIDE[axis]

    used = [0]

    def remote(src, dst, to):
        i = used[0]
        used[0] += 1
        copy = pltpu.make_async_remote_copy(
            src_ref=src, dst_ref=dst, send_sem=send_sems.at[i], recv_sem=recv_sems.at[i],
            device_id=(to,), device_id_type=MESH,
        )
        copy.start()
        return copy

    def add(target, row0, rows, terms):
        step = rows // 8 if rows % 64 == 0 else rows

        def body(s, carry):
            at = pl.ds(pl.multiple_of(s * step, 8), step)
            total = terms[0](at)
            for term in terms[1:]:
                total = total + term(at)
            target(at, total)
            return carry

        lax.fori_loop(0, rows // step, body, 0)

    def group_lanes(part, at_first, at_core):
        blocks = PARTS[part][0]
        block = BASE[part] + (at_core * 4 + at_first) * blocks
        return pl.ds(pl.multiple_of(block * LANES, LANES), blocks * LANES)

    local = []
    for p in range(3):
        copy = pltpu.make_async_copy(grads[p].at[core], own[p], local_sems.at[p])
        copy.start()
        local.append(copy)
    fetch = []
    for p, (blocks, axes) in enumerate(PARTS):
        copy = pltpu.make_async_copy(
            weights_t.at[:, group_lanes(p, where[axes[0]], core)], weight[p], local_sems.at[3 + p]
        )
        copy.start()
        fetch.append(copy)

    barrier = pltpu.get_barrier_semaphore()
    pl.semaphore_signal(barrier, inc=1, device_id=(sibling,), device_id_type=MESH)
    for axis in ("x", "z", "y"):
        for k in (1, 2, 3):
            pl.semaphore_signal(barrier, inc=1, device_id=(peer(axis, k),), device_id_type=MESH)
    pl.semaphore_wait(barrier, 10)

    halves = {}
    for k in (2, 1, 3, 0):
        for p, (blocks, axes) in enumerate(PARTS):
            at = ahead(axes[0], k)
            halves[k, p] = remote(grads[p].at[1 - core, at], pair[p].at[at], sibling)
    for copy in local:
        copy.wait()

    sent = []
    firsts = {}
    for k in (2, 1, 3, 0):
        for p, (blocks, axes) in enumerate(PARTS):
            at = ahead(axes[0], k)
            halves[k, p].wait_recv()
            rows = 16 * TILES[p] * 8
            mine, theirs = own[p], pair[p]

            def store(s, value, mine=mine, at=at):
                mine[at, s, :] = value

            add(store, 0, rows, [
                lambda s, mine=mine, at=at: mine[at, s, :],
                lambda s, theirs=theirs, at=at: theirs[at, s, :],
            ])
            if k:
                firsts[k, p] = remote(own[p].at[at], first[p].at[k - 1], peer(axes[0], k))

    seconds = {}
    for p, (blocks, axes) in enumerate(PARTS):
        at = where[axes[0]]
        for k in (1, 2, 3):
            firsts[k, p].wait_recv()
        rows = 16 * TILES[p] * 8
        mine, got = own[p], first[p]

        def store(s, value, mine=mine, at=at):
            mine[at, s, :] = value

        add(store, 0, rows, [lambda s, mine=mine, at=at: mine[at, s, :]] + [
            (lambda s, got=got, k=k: got[k, s, :]) for k in range(3)
        ])
        size = 4 * TILES[p] * 8
        for k in (2, 1, 3):
            rows_at = pl.ds(pl.multiple_of(ahead(axes[1], k) * size, 8), size)
            seconds[k, p] = remote(own[p].at[at, rows_at], second[p].at[k - 1], peer(axes[1], k))

    thirds = {}
    for p, (blocks, axes) in enumerate(PARTS):
        at = where[axes[0]]
        for k in (1, 2, 3):
            seconds[k, p].wait_recv()
        size = 4 * TILES[p] * 8
        base = where[axes[1]] * size
        mine, got = own[p], second[p]
        total = mine[at, pl.ds(pl.multiple_of(base, 8), size), :]
        for k in range(3):
            total = total + got[k]
        mine[at, pl.ds(pl.multiple_of(base, 8), size), :] = total
        small = TILES[p] * 8
        for k in (2, 1, 3):
            rows_at = pl.ds(pl.multiple_of(base + ahead(axes[2], k) * small, 8), small)
            thirds[k, p] = remote(own[p].at[at, rows_at], third[p].at[k - 1], peer(axes[2], k))

    backs = {}
    for p, (blocks, axes) in enumerate(PARTS):
        at = where[axes[0]]
        for k in (1, 2, 3):
            thirds[k, p].wait_recv()
        small = TILES[p] * 8
        row = where[axes[1]] * 4 + where[axes[2]]
        total = own[p][at, pl.ds(pl.multiple_of(row * small, 8), small), :]
        for k in range(3):
            total = total + third[p][k]
        full[p][row] = total
        for k in (2, 1, 3):
            backs[k, p] = remote(full[p].at[row], full[p].at[row], peer(axes[2], k))

    returns = {}
    for p, (blocks, axes) in enumerate(PARTS):
        for k in (1, 2, 3):
            backs[k, p].wait_recv()
        rows_at = pl.ds(where[axes[1]] * 4, 4)
        for k in (2, 1, 3):
            returns[k, p] = remote(full[p].at[rows_at], full[p].at[rows_at], peer(axes[1], k))

    lane = lax.broadcasted_iota(jnp.int32, (LANES, LANES), 1)
    lasts, across = {}, []
    stores = []
    for p, (blocks, axes) in enumerate(PARTS):
        for k in (1, 2, 3):
            returns[k, p].wait_recv()
        fetch[p].wait()
        tails = [full[p][:, (blocks + j) * 8 : (blocks + j) * 8 + 8, :].reshape(LANES, LANES) for j in range(3)]
        for block in range(blocks):
            head = full[p][:, block * 8 : block * 8 + 8, :].reshape(LANES, LANES)
            start = (TAIL * block) % LANES
            tile = (TAIL * block) // LANES
            tail = tails[tile]
            if start + TAIL > LANES:
                tail = jnp.where(lane >= start, tail, tails[tile + 1])
            if start:
                tail = pltpu.roll(tail, LANES - start, 1)
            grad = jnp.concatenate([head.T, tail.T[0:TAIL, :]], axis=0)
            lanes = slice(block * LANES, (block + 1) * LANES)
            at_block = BASE[p] + (core * 4 + where[axes[0]]) * blocks + block
            state = states[at_block] + jnp.sum(grad * grad, axis=0, keepdims=True) * (1.0 / D)
            new = weight[p][:, lanes] - learn_rate * grad / (jnp.sqrt(state) + epsilon)
            ready[p][0:D, lanes] = new
            ready[p][D:ROWS, lanes] = jnp.broadcast_to(state, (ROWS - D, LANES))
        place = group_lanes(p, where[axes[0]], core)
        for k in (2, 1, 3):
            lasts[k, p] = remote(ready[p], out.at[:, place], peer(axes[0], k))
        across.append(remote(ready[p], out.at[:, place], sibling))
        copy = pltpu.make_async_copy(ready[p], out.at[:, place], local_sems.at[6 + p])
        copy.start()
        stores.append(copy)

    for k in (1, 3, 2):
        for p, (blocks, axes) in enumerate(PARTS):
            lasts[k, p].wait_recv()
            place = group_lanes(p, ahead(axes[0], 4 - k), core)
            across.append(remote(out.at[:, place], out.at[:, place], sibling))
    for copy in across:
        copy.wait_recv()
    for copy in stores:
        copy.wait()
    for group in (halves, firsts, seconds, thirds, backs, returns, lasts):
        for copy in group.values():
            copy.wait_send()
    for copy in across:
        copy.wait_send()


def update_table(grads, weights_t, states):
    any_space = pl.BlockSpec(memory_space=pl.ANY)
    vmem = pl.BlockSpec(memory_space=pltpu.VMEM)
    rows = [16 * tiles * 8 for tiles in TILES]
    scratch = [pltpu.VMEM((4, r, LANES), F32) for r in rows] * 2
    scratch += [pltpu.VMEM((3, r, LANES), F32) for r in rows]
    scratch += [pltpu.VMEM((3, r // 4, LANES), F32) for r in rows]
    scratch += [pltpu.VMEM((3, r // 16, LANES), F32) for r in rows]
    scratch += [pltpu.VMEM((16, tiles * 8, LANES), F32) for tiles in TILES]
    scratch += [pltpu.VMEM((ROWS, n * LANES), F32) for n, _ in PARTS]
    scratch += [pltpu.VMEM((D, n * LANES), F32) for n, _ in PARTS]
    scratch += [
        pltpu.SemaphoreType.DMA((9,)),
        pltpu.SemaphoreType.DMA((78,)),
        pltpu.SemaphoreType.DMA((78,)),
    ]
    return pl.pallas_call(
        table_kernel,
        out_shape=jax.ShapeDtypeStruct((ROWS, REL), F32),
        in_specs=[any_space] * 4 + [vmem],
        out_specs=any_space,
        scratch_shapes=scratch,
        compiler_params=pltpu.CompilerParams(
            collective_id=0, has_side_effects=True, vmem_limit_bytes=40 << 20
        ),
        name="update_table",
    )(*grads, weights_t, states)


def swap_kernel(mask, block, out, send_sem, recv_sem):
    me = lax.axis_index("dev")
    partner = me
    for bit in range(7):
        if mask >> bit & 1:
            partner = partner + (1 << bit) * (1 - 2 * lax.rem(me // (1 << bit), 2))
    barrier = pltpu.get_barrier_semaphore()
    pl.semaphore_signal(barrier, inc=1, device_id=(partner,), device_id_type=MESH)
    pl.semaphore_wait(barrier, 1)
    copy = pltpu.make_async_remote_copy(
        src_ref=block, dst_ref=out, send_sem=send_sem, recv_sem=recv_sem,
        device_id=(partner,), device_id_type=MESH,
    )
    copy.start()
    copy.wait()


def swap(mask):
    return pl.pallas_call(
        functools.partial(swap_kernel, mask),
        out_shape=jax.ShapeDtypeStruct((D, NODES), F32),
        in_specs=[pl.BlockSpec(memory_space=pl.ANY)],
        out_specs=pl.BlockSpec(memory_space=pl.ANY),
        scratch_shapes=[pltpu.SemaphoreType.DMA, pltpu.SemaphoreType.DMA],
        compiler_params=pltpu.CompilerParams(
            collective_id=mask, has_side_effects=True, vmem_limit_bytes=8 << 20
        ),
        name="swap",
    )


def exchange(payload, flip_mask):
    def node(mask, bits):
        if bits == 0:
            return swap(mask) if mask else lambda block: block
        bit = bits - 1
        high, low = node(mask | 1 << bit, bit), node(mask, bit)
        return lambda block: lax.cond(
            jnp.bitwise_and(jnp.right_shift(flip_mask, bit), 1) == 1, high, low, block
        )

    return node(0, 7)(payload)


def shards(
    embeddings,
    node_state,
    relations,
    relation_state,
    plan,
    edge_count,
    sources,
    targets,
    relation_ids,
    negatives,
):
    flip_mask = plan[0]
    left_t = embeddings.T
    table_t = relations.T
    rel_rows = gather_rows(relation_ids, table_t)
    right_t = exchange(left_t, flip_mask)
    left_grad, right_grad, *packed = bucket_gradients(
        relation_ids, edge_count, left_t, right_t, rel_rows, sources, targets, negatives
    )
    grads = [
        g.reshape(2, 4, 16 * tiles * 8, LANES) for g, tiles in zip(packed, TILES)
    ]
    returned = exchange(right_grad, flip_mask)
    table = update_table(grads, table_t, relation_state.reshape(REL // LANES, 1, LANES))

    node_grad = left_grad + returned
    new_node_state = node_state + jnp.mean(node_grad * node_grad, axis=0)
    new_left = left_t - learn_rate * node_grad / (jnp.sqrt(new_node_state)[None, :] + epsilon)
    return (new_left.T, new_node_state, table[0:D].T, table[D])


def solution(mesh):
    return jax.shard_map(
        shards,
        mesh=mesh,
        in_specs=(
            P("dev", None),
            P("dev"),
            P(),
            P(),
            P(),
            P("dev"),
            P("dev"),
            P("dev"),
            P("dev"),
            P("dev", None),
        ),
        out_specs=(P("dev", None), P("dev"), P(), P()),
        check_vma=False,
    )
```

```python
import functools

import jax
import jax.numpy as jnp
from jax import lax
from jax.experimental import pallas as pl
from jax.experimental.pallas import tpu as pltpu
from jax.sharding import PartitionSpec as P

learn_rate = 0.1
epsilon = 1e-06

F32 = jnp.float32
BF16 = jnp.bfloat16
MESH = pl.DeviceIdType.MESH
D = 200
WIDE = 256
REL = 14336
NODES = 1024
EDGES = 2048
LANES = 128
TAIL = D - LANES
CHUNK = 256
TABLE_STEP = 1024

PARTS = ((5, ("x", "z", "y")), (5, ("z", "y", "x")), (4, ("y", "x", "z")))
STRIDE = {"x": 32, "z": 8, "y": 2}
TILES = tuple(n + 3 for n, _ in PARTS)
BASE = (0, 40, 80)
ROWS = 208


def split2(x):
    high = x.astype(BF16)
    return high, (x - high.astype(F32)).astype(BF16)


def dot(a, b):
    return jnp.dot(a, b, preferred_element_type=F32)


def dot_nt(a, b):
    return lax.dot_general(a, b, (((1,), (1,)), ((), ())), preferred_element_type=F32)


def gather_rows(ids, table_t, rows, buf, table, sems):
    def load(j):
        lanes = pl.ds(pl.multiple_of(j * TABLE_STEP, TABLE_STEP), TABLE_STEP)
        return pltpu.make_async_copy(table_t.at[:, lanes], buf.at[j], sems.at[j])

    def begin(j, carry):
        load(j).start()
        return carry

    lax.fori_loop(0, REL // TABLE_STEP, begin, 0)

    def turn(j, carry):
        load(j).wait()

        def block(b, carry):
            lanes = pl.ds(pl.multiple_of(b * LANES, LANES), LANES)
            at = pl.ds(pl.multiple_of(j * TABLE_STEP + b * LANES, LANES), LANES)
            table[at, 0:LANES] = buf[j, 0:LANES, lanes].T
            low = jnp.concatenate(
                [buf[j, LANES:D, lanes], jnp.zeros((WIDE - D, LANES), F32)], axis=0
            )
            table[at, LANES:WIDE] = low.T
            return carry

        lax.fori_loop(0, TABLE_STEP // LANES, block, 0)
        return carry

    lax.fori_loop(0, REL // TABLE_STEP, turn, 0)

    def fetch(step, carry):
        first = pl.multiple_of(step * 16, 16)
        for k in range(16):
            rows[pl.ds(first + k, 1), :] = table[pl.ds(ids[first + k], 1), :]
        return carry

    lax.fori_loop(0, EDGES // 16, fetch, 0)


def column(row):
    return jnp.broadcast_to(row, (LANES, LANES)).T


def one_hot_pieces(row, width):
    ids = column(row)
    lane = lax.broadcasted_iota(jnp.int32, (LANES, LANES), 1)
    return [ids == lane + j * LANES for j in range(width // LANES)]


def one_hot(rows):
    return jnp.concatenate(
        [jnp.concatenate(one_hot_pieces(row, NODES), axis=1) for row in rows], axis=0
    )


def gradient_kernel(
    ids, live, left_t, right_t, rel_rows, sources, targets, negatives,
    left_grad, right_grad, g0, g1, g2,
    left_hi, left_lo, right_hi, right_lo, counts, rel_grad, table,
):
    def clear(step, carry):
        table[pl.ds(pl.multiple_of(step * 512, 512), 512), :] = jnp.zeros((512, WIDE), F32)
        return carry

    lax.fori_loop(0, REL // 512, clear, 0)

    pad = jnp.zeros((WIDE - D, NODES), BF16)
    for source, hi, lo in ((left_t, left_hi, left_lo), (right_t, right_hi, right_lo)):
        high, low = split2(source[...])
        hi[0:D, :] = high
        lo[0:D, :] = low
        hi[D:WIDE, :] = pad
        lo[D:WIDE, :] = pad
    left_grad[...] = jnp.zeros_like(left_grad)
    right_grad[...] = jnp.zeros_like(right_grad)

    for span in range(2):
        counts[span : span + 1, :] = jnp.zeros((1, NODES), F32)

        def count(k, carry):
            pieces = one_hot_pieces(negatives[pl.ds(span * 8 + k, 1), :], NODES)
            counts[span : span + 1, :] += jnp.concatenate(
                [jnp.sum(p.astype(F32), axis=0, keepdims=True) for p in pieces], axis=1
            )
            return carry

        lax.fori_loop(0, 8, count, 0)

    def chunk(step, carry):
        first = pl.multiple_of(step * CHUNK, CHUNK)
        edges = pl.ds(first, CHUNK)
        source_hot = one_hot([sources[pl.ds(step * 2 + h, 1), :] for h in range(2)])
        target_hot = one_hot([targets[pl.ds(step * 2 + h, 1), :] for h in range(2)])
        from_source = source_hot.astype(F32).astype(BF16)
        from_target = target_hot.astype(F32)

        rel = rel_rows[edges, :]
        left = dot_nt(from_source, left_hi[...]) + dot_nt(from_source, left_lo[...])
        query = left * rel
        q_hi, q_lo = split2(query)
        score = (
            dot(q_hi, right_hi[...]) + dot(q_hi, right_lo[...]) + dot(q_lo, right_hi[...])
        )

        span = step // (NODES // CHUNK)
        weight = counts[pl.ds(span, 1), :] + from_target
        score = jnp.where(weight > 0, score, -3e38)
        top = jnp.max(score, axis=1, keepdims=True)
        grown = weight * jnp.exp(score - top)
        total = jnp.sum(grown, axis=1, keepdims=True)
        slot = first + lax.broadcasted_iota(jnp.int32, (CHUNK, 1), 0)
        alive = (slot < live[0]).astype(F32)
        grad = grown * (alive / total) - from_target * alive

        d_hi, d_lo = split2(grad)
        d_query = (
            dot_nt(d_hi, right_hi[...]) + dot_nt(d_lo, right_hi[...]) + dot_nt(d_hi, right_lo[...])
        )
        rel_grad[edges, :] = d_query * left
        d_left = d_query * rel
        query_t = query.T[0:D, :]
        qt_hi, qt_lo = split2(query_t)
        right_grad[...] += dot(qt_hi, d_hi) + dot(qt_lo, d_hi) + dot(qt_hi, d_lo)
        lt_hi, lt_lo = split2(d_left.T[0:D, :])
        left_grad[...] += dot(lt_hi, from_source) + dot(lt_lo, from_source)
        return carry

    lax.fori_loop(0, EDGES // CHUNK, chunk, 0)

    def scatter(step, carry):
        first = pl.multiple_of(step * 16, 16)
        for k in range(16):
            at = pl.ds(ids[first + k], 1)
            table[at, :] += rel_grad[pl.ds(first + k, 1), :]
        return carry

    lax.fori_loop(0, EDGES // 16, scatter, 0)

    lane = lax.broadcasted_iota(jnp.int32, (LANES, LANES), 1)
    for part, out in enumerate((g0, g1, g2)):
        blocks = PARTS[part][0]

        def pack(group, carry):
            tails = []
            for block in range(blocks):
                at = pl.ds(
                    pl.multiple_of((BASE[part] + group * blocks + block) * LANES, LANES), LANES
                )
                out[group, :, block * 8 : block * 8 + 8, :] = table[at, 0:LANES].reshape(16, 8, LANES)
                tail = table[at, LANES:WIDE]
                tails.append(pltpu.roll(tail, (TAIL * block) % LANES, 1) if block else tail)
            packed = [
                tails[0] + jnp.where(lane >= 72, tails[1], 0.0),
                jnp.where(lane < 16, tails[1], 0.0) + tails[2] + jnp.where(lane >= 88, tails[3], 0.0),
                jnp.where(lane < 32, tails[3], 0.0),
            ]
            if blocks == 5:
                packed[2] = packed[2] + tails[4]
            for j in range(3):
                at = (blocks + j) * 8
                out[group, :, at : at + 8, :] = packed[j].reshape(16, 8, LANES)
            return carry

        lax.fori_loop(0, 8, pack, 0)


def bucket_gradients(relation_ids, live, left_t, right_t, rel_rows, sources, targets, negatives):
    vmem = pl.BlockSpec(memory_space=pltpu.VMEM)
    smem = pl.BlockSpec(memory_space=pltpu.SMEM)
    packed = [pltpu.VMEM((8, 16, tiles * 8, LANES), F32) for tiles in TILES]
    return pl.pallas_call(
        gradient_kernel,
        out_shape=[
            jax.ShapeDtypeStruct((D, NODES), F32),
            jax.ShapeDtypeStruct((D, NODES), F32),
            *packed,
        ],
        in_specs=[smem, smem] + [vmem] * 6,
        out_specs=[vmem] * 5,
        scratch_shapes=[
            pltpu.VMEM((WIDE, NODES), BF16),
            pltpu.VMEM((WIDE, NODES), BF16),
            pltpu.VMEM((WIDE, NODES), BF16),
            pltpu.VMEM((WIDE, NODES), BF16),
            pltpu.VMEM((2, NODES), F32),
            pltpu.VMEM((EDGES, WIDE), F32),
            pltpu.VMEM((REL, WIDE), F32),
        ],
        compiler_params=pltpu.CompilerParams(vmem_limit_bytes=30 << 20),
        name="bucket_gradients",
    )(
        relation_ids, live, left_t, right_t, rel_rows,
        sources.reshape(16, LANES), targets.reshape(16, LANES), negatives.reshape(16, LANES),
    )


def table_kernel(
    g0, g1, g2, weights_t, states, out,
    pair0, pair1, pair2, relay0, relay1, relay2, r10, r11, r12, r20, r21, r22, r30, r31, r32,
    f0, f1, f2, c0, c1, c2, w0, w1, w2, local_sems, send_sems, recv_sems,
):
    me = lax.axis_index("dev")
    core = lax.rem(me, 2)
    where = {"y": lax.rem(me // 2, 4), "z": lax.rem(me // 8, 4), "x": me // 32}
    sibling = me + 1 - 2 * core
    grads, pair, relay = (g0, g1, g2), (pair0, pair1, pair2), (relay0, relay1, relay2)
    first, second, third = (r10, r11, r12), (r20, r21, r22), (r30, r31, r32)
    full, ready, weight = (f0, f1, f2), (c0, c1, c2), (w0, w1, w2)
    parts = [(p, blocks, axes) for p, (blocks, axes) in enumerate(PARTS)]

    def ahead(axis, k):
        return lax.rem(where[axis] + k, 4)

    def peer(axis, k):
        return me + (ahead(axis, k) - where[axis]) * STRIDE[axis]

    sent = []

    def remote(src, dst, to):
        i = len(sent)
        copy = pltpu.make_async_remote_copy(
            src_ref=src, dst_ref=dst, send_sem=send_sems.at[i], recv_sem=recv_sems.at[i],
            device_id=(to,), device_id_type=MESH,
        )
        copy.start()
        sent.append(copy)
        return copy

    def add(rows, start, target, terms):
        steps = 8 if rows % 64 == 0 else 4
        step = rows // steps
        assert step % 8 == 0

        def body(s, carry):
            here = pl.ds(pl.multiple_of(s * step, 8), step)
            there = pl.ds(pl.multiple_of(start + s * step, 8), step)
            total = target[there, :]
            for term in terms:
                total = total + term[here, :]
            target[there, :] = total
            return carry

        lax.fori_loop(0, steps, body, 0)

    def group_lanes(part, at_first, at_core):
        blocks = PARTS[part][0]
        block = BASE[part] + (at_core * 4 + at_first) * blocks
        return pl.ds(pl.multiple_of(block * LANES, LANES), blocks * LANES)

    fetch = []
    for p, blocks, axes in parts:
        copy = pltpu.make_async_copy(
            weights_t.at[:, group_lanes(p, where[axes[0]], core)], weight[p], local_sems.at[p]
        )
        copy.start()
        fetch.append(copy)

    barrier = pltpu.get_barrier_semaphore()
    pl.semaphore_signal(barrier, inc=1, device_id=(sibling,), device_id_type=MESH)
    for axis in ("x", "z", "y"):
        for k in (1, 2, 3):
            pl.semaphore_signal(barrier, inc=1, device_id=(peer(axis, k),), device_id_type=MESH)
    pl.semaphore_wait(barrier, 10)

    halves = {}
    for k in (2, 1, 3, 0):
        for p, blocks, axes in parts:
            at = ahead(axes[0], k)
            halves[k, p] = remote(grads[p].at[1 - core, at], pair[p].at[at], sibling)

    relays, parcels = {}, []
    for k in (2, 1, 3, 0):
        for p, blocks, axes in parts:
            at = ahead(axes[0], k)
            halves[k, p].wait_recv()
            rows = 16 * TILES[p] * 8
            half = rows // 2
            add(rows, 0, pair[p].at[at], [grads[p].at[core, at]])
            top, bottom = pl.ds(0, half), pl.ds(half, half)
            if k == 2:
                relays[1, p] = remote(pair[p].at[at, top], relay[p].at[0], peer(axes[0], 1))
                relays[3, p] = remote(pair[p].at[at, bottom], relay[p].at[1], peer(axes[0], 3))
            if k == 1:
                parcels.append((p, remote(pair[p].at[at, bottom], first[p].at[0, bottom], peer(axes[0], 1))))
            if k == 3:
                parcels.append((p, remote(pair[p].at[at, top], first[p].at[1, top], peer(axes[0], 3))))
    for p, blocks, axes in parts:
        half = 8 * TILES[p] * 8
        top, bottom = pl.ds(0, half), pl.ds(half, half)
        at = ahead(axes[0], 1)
        relays[1, p].wait_recv()
        add(half, 0, pair[p].at[at], [relay[p].at[0]])
        parcels.append((p, remote(pair[p].at[at, top], first[p].at[0, top], peer(axes[0], 1))))
        at = ahead(axes[0], 3)
        relays[3, p].wait_recv()
        add(half, half, pair[p].at[at], [relay[p].at[1]])
        parcels.append((p, remote(pair[p].at[at, bottom], first[p].at[1, bottom], peer(axes[0], 3))))

    seconds = {}
    for p, blocks, axes in parts:
        at = where[axes[0]]
        for q, copy in parcels:
            if q == p:
                copy.wait_recv()
        add(16 * TILES[p] * 8, 0, pair[p].at[at], [first[p].at[0], first[p].at[1]])
        size = 4 * TILES[p] * 8
        for k in (2, 1, 3):
            rows_at = pl.ds(pl.multiple_of(ahead(axes[1], k) * size, 8), size)
            seconds[k, p] = remote(pair[p].at[at, rows_at], second[p].at[k - 1], peer(axes[1], k))

    thirds = {}
    for p, blocks, axes in parts:
        at = where[axes[0]]
        for k in (1, 2, 3):
            seconds[k, p].wait_recv()
        size = 4 * TILES[p] * 8
        base = where[axes[1]] * size
        add(size, base, pair[p].at[at], [second[p].at[k] for k in range(3)])
        small = TILES[p] * 8
        for k in (2, 1, 3):
            rows_at = pl.ds(pl.multiple_of(base + ahead(axes[2], k) * small, 8), small)
            thirds[k, p] = remote(pair[p].at[at, rows_at], third[p].at[k - 1], peer(axes[2], k))

    backs = {}
    for p, blocks, axes in parts:
        at = where[axes[0]]
        for k in (1, 2, 3):
            thirds[k, p].wait_recv()
        small = TILES[p] * 8
        row = where[axes[1]] * 4 + where[axes[2]]
        total = pair[p][at, pl.ds(pl.multiple_of(row * small, 8), small), :]
        for k in range(3):
            total = total + third[p][k]
        full[p][row] = total
        for k in (2, 1, 3):
            backs[k, p] = remote(full[p].at[row], full[p].at[row], peer(axes[2], k))

    returns = {}
    for p, blocks, axes in parts:
        for k in (1, 2, 3):
            backs[k, p].wait_recv()
        rows_at = pl.ds(where[axes[1]] * 4, 4)
        for k in (2, 1, 3):
            returns[k, p] = remote(full[p].at[rows_at], full[p].at[rows_at], peer(axes[1], k))

    lane = lax.broadcasted_iota(jnp.int32, (LANES, LANES), 1)
    top, bottom = pl.ds(0, ROWS // 2), pl.ds(ROWS // 2, ROWS // 2)
    arrivals, across, stores = {}, [], []
    for p, blocks, axes in parts:
        for k in (1, 2, 3):
            returns[k, p].wait_recv()
        fetch[p].wait()

        def update(block, carry, p=p, blocks=blocks, axes=axes):
            head = full[p][:, pl.ds(pl.multiple_of(block * 8, 8), 8), :].reshape(LANES, LANES)
            start = lax.rem(TAIL * block, LANES)
            tile = (TAIL * block) // LANES
            after = jnp.minimum(tile + 1, 2)
            tail = full[p][:, pl.ds(pl.multiple_of((blocks + tile) * 8, 8), 8), :].reshape(LANES, LANES)
            more = full[p][:, pl.ds(pl.multiple_of((blocks + after) * 8, 8), 8), :].reshape(LANES, LANES)
            tail = pltpu.roll(jnp.where(lane >= start, tail, more), lax.rem(LANES - start, LANES), 1)
            grad = jnp.concatenate([head.T, tail.T[0:TAIL, :]], axis=0)
            lanes = pl.ds(pl.multiple_of(block * LANES, LANES), LANES)
            state = states[BASE[p] + (core * 4 + where[axes[0]]) * blocks + block]
            state = state + jnp.sum(grad * grad, axis=0, keepdims=True) * (1.0 / D)
            new = weight[p][:, lanes] - learn_rate * grad / (jnp.sqrt(state) + epsilon)
            ready[p][0:D, lanes] = new
            ready[p][D:ROWS, lanes] = jnp.broadcast_to(state, (ROWS - D, LANES))
            return carry

        lax.fori_loop(0, blocks, update, 0)
        place = group_lanes(p, where[axes[0]], core)
        for side, order in ((1, (top, bottom)), (3, (bottom, top))):
            for i, rows in enumerate(order):
                arrivals[side, i, p] = remote(
                    ready[p].at[rows, :], out.at[rows, place], peer(axes[0], side)
                )
        across.append(remote(ready[p], out.at[:, place], sibling))
        copy = pltpu.make_async_copy(ready[p], out.at[:, place], local_sems.at[3 + p])
        copy.start()
        stores.append(copy)

    distant = {}
    for p, blocks, axes in parts:
        for side, rows in ((1, top), (3, bottom)):
            arrivals[side, 0, p].wait_recv()
            place = group_lanes(p, ahead(axes[0], 4 - side), core)
            distant[side, p] = remote(out.at[rows, place], out.at[rows, place], peer(axes[0], side))
    for p, blocks, axes in parts:
        for side in (1, 3):
            arrivals[side, 1, p].wait_recv()
            place = group_lanes(p, ahead(axes[0], 4 - side), core)
            across.append(remote(out.at[:, place], out.at[:, place], sibling))
    for p, blocks, axes in parts:
        distant[1, p].wait_recv()
        distant[3, p].wait_recv()
        place = group_lanes(p, ahead(axes[0], 2), core)
        across.append(remote(out.at[:, place], out.at[:, place], sibling))
    for copy in across:
        copy.wait_recv()
    for copy in stores:
        copy.wait()
    for copy in sent:
        copy.wait_send()


def update_table(grads, weights_t, states):
    vmem = pl.BlockSpec(memory_space=pltpu.VMEM)
    rows = [16 * tiles * 8 for tiles in TILES]
    scratch = [pltpu.VMEM((4, r, LANES), F32) for r in rows]
    scratch += [pltpu.VMEM((2, r // 2, LANES), F32) for r in rows]
    scratch += [pltpu.VMEM((2, r, LANES), F32) for r in rows]
    scratch += [pltpu.VMEM((3, r // 4, LANES), F32) for r in rows]
    scratch += [pltpu.VMEM((3, r // 16, LANES), F32) for r in rows]
    scratch += [pltpu.VMEM((16, tiles * 8, LANES), F32) for tiles in TILES]
    scratch += [pltpu.VMEM((ROWS, n * LANES), F32) for n, _ in PARTS]
    scratch += [pltpu.VMEM((D, n * LANES), F32) for n, _ in PARTS]
    scratch += [
        pltpu.SemaphoreType.DMA((6,)),
        pltpu.SemaphoreType.DMA((96,)),
        pltpu.SemaphoreType.DMA((96,)),
    ]
    return pl.pallas_call(
        table_kernel,
        out_shape=pltpu.VMEM((ROWS, REL), F32),
        in_specs=[vmem] * 3 + [pl.BlockSpec(memory_space=pl.ANY), vmem],
        out_specs=vmem,
        scratch_shapes=scratch,
        compiler_params=pltpu.CompilerParams(
            collective_id=0, has_side_effects=True, vmem_limit_bytes=29 << 20
        ),
        name="update_table",
    )(*grads, weights_t, states)


def finish_kernel(table, weights, states, sems):
    copies = [pltpu.make_async_copy(table.at[pl.ds(D, 1)], states, sems.at[5])]
    for i in range(5):
        rows = pl.ds(i * 40, 40)
        copies.append(pltpu.make_async_copy(table.at[rows], weights.at[rows], sems.at[i]))
    for copy in copies:
        copy.start()
    for copy in copies:
        copy.wait()


def finish(table):
    any_space = pl.BlockSpec(memory_space=pl.ANY)
    return pl.pallas_call(
        finish_kernel,
        out_shape=[
            jax.ShapeDtypeStruct((D, REL), F32),
            jax.ShapeDtypeStruct((1, REL), F32),
        ],
        in_specs=[any_space],
        out_specs=[any_space] * 2,
        scratch_shapes=[pltpu.SemaphoreType.DMA((6,))],
        compiler_params=pltpu.CompilerParams(vmem_limit_bytes=1 << 20),
        name="finish",
    )(table)


def partner_of(me, mask):
    partner, bit = me, 0
    while mask >> bit:
        width = 0
        while mask >> (bit + width) & 1:
            width += 1
        if width:
            field = lax.rem(me // (1 << bit), 1 << width)
            partner = partner + (((1 << width) - 1) - 2 * field) * (1 << bit)
        bit += width + 1
    return partner


def swap_start(mask, block, out, send_sem, recv_sem):
    partner = partner_of(lax.axis_index("dev"), mask)
    barrier = pltpu.get_barrier_semaphore()
    pl.semaphore_signal(barrier, inc=1, device_id=(partner,), device_id_type=MESH)
    pl.semaphore_wait(barrier, 1)
    copy = pltpu.make_async_remote_copy(
        src_ref=block, dst_ref=out, send_sem=send_sem, recv_sem=recv_sem,
        device_id=(partner,), device_id_type=MESH,
    )
    copy.start()
    return copy


def fetch_kernel(mask, block, ids, table_t, out, rows, send_sem, recv_sem, buf, table, sems):
    copy = swap_start(mask, block, out, send_sem, recv_sem)
    gather_rows(ids, table_t, rows, buf, table, sems)
    copy.wait()


def return_kernel(mask, block, out, send_sem, recv_sem):
    swap_start(mask, block, out, send_sem, recv_sem).wait()


ANY = pl.BlockSpec(memory_space=pl.ANY)
ROWS_SPEC = pl.BlockSpec(memory_space=pltpu.VMEM)
GATHER_SCRATCH = [
    pltpu.VMEM((REL // TABLE_STEP, D, TABLE_STEP), F32),
    pltpu.VMEM((REL, WIDE), F32),
    pltpu.SemaphoreType.DMA((REL // TABLE_STEP,)),
]


def fetch(mask):
    if mask == 0:
        return lambda block, ids, table_t: (block, pick(ids, table_t))
    return pl.pallas_call(
        functools.partial(fetch_kernel, mask),
        out_shape=[
            jax.ShapeDtypeStruct((D, NODES), F32),
            jax.ShapeDtypeStruct((EDGES, WIDE), F32),
        ],
        in_specs=[ANY, pl.BlockSpec(memory_space=pltpu.SMEM), ANY],
        out_specs=[ANY, ROWS_SPEC],
        scratch_shapes=[pltpu.SemaphoreType.DMA, pltpu.SemaphoreType.DMA, *GATHER_SCRATCH],
        compiler_params=pltpu.CompilerParams(
            collective_id=128 + mask, has_side_effects=True, vmem_limit_bytes=48 << 20
        ),
        name="fetch",
    )


def pick(ids, table_t):
    return pl.pallas_call(
        gather_rows,
        out_shape=jax.ShapeDtypeStruct((EDGES, WIDE), F32),
        in_specs=[pl.BlockSpec(memory_space=pltpu.SMEM), ANY],
        out_specs=ROWS_SPEC,
        scratch_shapes=GATHER_SCRATCH,
        compiler_params=pltpu.CompilerParams(vmem_limit_bytes=48 << 20),
        name="pick",
    )(ids, table_t)


def swap(mask):
    if mask == 0:
        return lambda block: block
    return pl.pallas_call(
        functools.partial(return_kernel, mask),
        out_shape=jax.ShapeDtypeStruct((D, NODES), F32),
        in_specs=[ANY],
        out_specs=ANY,
        scratch_shapes=[pltpu.SemaphoreType.DMA, pltpu.SemaphoreType.DMA],
        compiler_params=pltpu.CompilerParams(
            collective_id=mask, has_side_effects=True, vmem_limit_bytes=8 << 20
        ),
        name="swap",
    )


def with_partner(leaf, flip_mask, bits, *operands):
    low, count = bits
    branches = [leaf(k << low) for k in range(1 << count)]
    choice = jnp.bitwise_and(jnp.right_shift(flip_mask, low), (1 << count) - 1)
    return lax.switch(choice, branches, *operands)


FAR, NEAR = (3, 4), (0, 3)


def shards(
    embeddings,
    node_state,
    relations,
    relation_state,
    plan,
    edge_count,
    sources,
    targets,
    relation_ids,
    negatives,
):
    flip_mask = plan[0]
    left_t = embeddings.T
    table_t = relations.T
    right_t, rel_rows = with_partner(fetch, flip_mask, FAR, left_t, relation_ids, table_t)
    right_t = with_partner(swap, flip_mask, NEAR, right_t)
    left_grad, right_grad, *packed = bucket_gradients(
        relation_ids, edge_count, left_t, right_t, rel_rows, sources, targets, negatives
    )
    grads = [
        g.reshape(2, 4, 16 * tiles * 8, LANES) for g, tiles in zip(packed, TILES)
    ]
    table = update_table(grads, table_t, relation_state.reshape(REL // LANES, 1, LANES))
    new_table, new_states = finish(table)
    right_grad, new_table = lax.optimization_barrier((right_grad, new_table))
    returned = with_partner(swap, flip_mask, NEAR, right_grad)
    returned = with_partner(swap, flip_mask, FAR, returned)

    node_grad = left_grad + returned
    new_node_state = node_state + jnp.mean(node_grad * node_grad, axis=0)
    new_left = left_t - learn_rate * node_grad / (jnp.sqrt(new_node_state)[None, :] + epsilon)
    return (new_left.T, new_node_state, new_table.T, new_states.reshape(REL))


def solution(mesh):
    return jax.shard_map(
        shards,
        mesh=mesh,
        in_specs=(
            P("dev", None),
            P("dev"),
            P(),
            P(),
            P(),
            P("dev"),
            P("dev"),
            P("dev"),
            P("dev"),
            P("dev", None),
        ),
        out_specs=(P("dev", None), P("dev"), P(), P()),
        check_vma=False,
    )
```
